32 devices in a mesh: tok: 8 (over z, x), head: 4 (over y, core).
Axes of the slice: x: 2, y: 2, z: 4, core: 2. Of those that a mesh axis runs over, the one named last changes fastest.
Arguments:
- queries_first: bfloat16 [2048, 3072], P('tok', 'head'), may hold values from -180 to 180
- queries_second: bfloat16 [2048, 3072], P('tok', 'head'), may hold values from -180 to 180
- grads_first: bfloat16 [2048, 3072], P('tok', 'head'), may hold values from -6 to 6
- grads_second: bfloat16 [2048, 3072], P('tok', 'head'), may hold values from -6 to 6
- key_states: bfloat16 [2048, 1024], P('tok', 'head'), may hold values from -4.5 to 4.5
- value_states: bfloat16 [2048, 1024], P('tok', 'head'), may hold values from -6 to 6
- doc_lengths: int32 [8], replicated, may hold values from 1 to 768, 2048 in all
- hidden_states: bfloat16 [2048, 3072], P('tok', 'head'), may hold values from -6 to 6
Outputs:
- grad_queries_first: bfloat16 [2048, 3072], P('tok', 'head')
- grad_queries_second: bfloat16 [2048, 3072], P('tok', 'head')
- weight_grad: float32 [3072, 2048], P('tok', 'head')
The draws below stay inside these ranges and needn't reach their ends.
All inputs are finite; a program needn't handle non-finite values.
Results may differ from the reference program's by a relative error of at most 0.0075.
Values may be sent and summed in bfloat16 or wider, within the bound.
No kernel may reach another device: no remote copies, remote signals or barrier semaphores. Data moves between devices by JAX's collectives and lax.ppermute only.
A program may use at most 64 MiB of HBM per device.

```python
import math
import jax
import jax.numpy as jnp
import numpy as np
from jax import lax

D = 3072
QH = 24
KVH = 8
HD = 128
TOK_DEV = 256
REACH = 3
SEQ = 2048
DOC_MAX = 768
NDOCS = 8


def shared_keys(key):
    drawn = jnp.clip(jax.random.normal(jax.random.fold_in(key, 101), (SEQ, KVH * HD), jnp.float32), -4.5, 4.5)
    return drawn


def drawn_queries(key, offset):
    entries = jnp.clip(jax.random.normal(jax.random.fold_in(key, offset), (SEQ, QH * HD), jnp.float32), -4.5, 4.5)
    return entries


def draw_key_states(key, part):
    return shared_keys(key).astype(jnp.bfloat16)


def draw_queries_first(key, part):
    return drawn_queries(key, 201).astype(jnp.bfloat16)


def draw_queries_second(key, part):
    return drawn_queries(key, 202).astype(jnp.bfloat16)


def spiked(result, rng, source, target, shards_of, factor):
    def block_of(axis_at):
        return (jnp.arange(result.shape[axis_at]) // (result.shape[axis_at] // shards_of)).reshape((-1,) + (1,) * (result.ndim - 1 - axis_at))

    first = jax.random.permutation(rng, shards_of)[block_of(target)]
    far = (block_of(target) + shards_of // 2) % shards_of
    return jnp.where((block_of(source) == first) | (block_of(source) == far), factor * result, result)


def block_levels(key, dims, cuts, least, largest):
    def one(axis_at, blocks):
        heights = jax.random.uniform(jax.random.fold_in(jax.random.fold_in(key, 6), axis_at), (blocks,), jnp.float32, least / len(cuts), largest / len(cuts))
        return jnp.repeat(jnp.exp(heights), dims[axis_at] // blocks).reshape((-1,) + (1,) * (len(dims) - axis_at - 1))

    level = one(*cuts[0])
    for cut in cuts[1:]:
        level = level * one(*cut)
    return level


def split_up(number_of, total, limit, skew):
    loads = [(1 << 20) // math.isqrt(standing ** skew) + 1 for standing in range(2, number_of + 1)]
    surplus, counts = total - limit - (number_of - 1), [1] * (number_of - 1)
    while surplus > 0:
        candidates = [i for i in range(number_of - 1) if counts[i] < limit]
        whole, budget = sum([loads[i] for i in candidates]), surplus
        for i in candidates:
            more = min(limit - counts[i], max(1, budget * loads[i] // whole), surplus)
            counts[i] = counts[i] + more
            surplus = surplus - more
    return np.array([limit] + counts)


def ragged(key, count, total, limit, slope):
    if count == 2:
        one = jax.random.randint(key, (), max(1, total - limit), min(limit, total - 1) + 1)
        return jnp.stack([one, total - one])
    lengths = jnp.asarray(split_up(count, total, limit, slope), jnp.int32)
    twos = (count - 1) // 2
    source_of, taker = lengths[1:1 + 2 * twos:2], lengths[2:2 + 2 * twos:2]
    slack = jnp.minimum(source_of - 1, limit - taker)
    passed = jax.random.randint(jax.random.fold_in(key, 1), (twos,), 0, 1 << 20) % (slack + 1)
    lengths = lengths.at[1:1 + 2 * twos:2].set(source_of - passed).at[2:2 + 2 * twos:2].set(taker + passed)
    return lengths[jax.random.permutation(jax.random.fold_in(key, 2), count)]


def normal_values(own_key, shape, scale, most, split=(), held_as=jnp.bfloat16):
    entries = scale * jax.random.normal(own_key, shape, jnp.float32)
    if split:
        entries = entries * block_levels(own_key, shape, split, -0.22, 0.18)
    return jnp.clip(entries, -most, most).astype(held_as)


def heavy_noise(key, extent, scale, reach, shards, heavy, held_as=jnp.bfloat16):
    values = scale * jax.random.normal(key, extent, jnp.float32)
    if shards:
        values = values * block_levels(key, extent, shards, -0.22, 0.18)
    return jnp.clip(spiked(values, jax.random.fold_in(key, 3), *heavy), -reach, reach).astype(held_as)


def setup_inputs(seed: int = 0) -> dict:
    splits = jax.random.split(jax.random.key(seed), 9)
    return {
        "queries_first": draw_queries_first(jax.random.fold_in(splits[8], 71), 0),
        "queries_second": draw_queries_second(jax.random.fold_in(splits[8], 71), 0),
        "grads_first": normal_values(splits[2], (SEQ, QH * HD), 1.0, 6.0, ((0, 8), (1, 4))),
        "grads_second": normal_values(splits[3], (SEQ, QH * HD), 1.0, 6.0, ((0, 8), (1, 4))),
        "key_states": draw_key_states(jax.random.fold_in(splits[8], 71), 0),
        "value_states": normal_values(splits[5], (SEQ, KVH * HD), 1.0, 6.0, ((0, 8), (1, 4))),
        "doc_lengths": ragged(splits[6], NDOCS, SEQ, DOC_MAX, 2).astype(jnp.int32),
        "hidden_states": heavy_noise(splits[7], (SEQ, D), 1.0, 6.0, ((0, 8), (1, 4)), (0, 1, 8, 2.0)),
    }


def document_of(places, doc_ends):
    return lax.optimization_barrier(jnp.sum((places[:, None] >= doc_ends[None, :]).astype(jnp.int32), axis=1))

def causal_mask(query_places, key_places, doc_ends):
    same_doc = document_of(query_places, doc_ends)[:, None] == document_of(jnp.maximum(key_places, 0), doc_ends)[None, :]
    return same_doc & (key_places[None, :] <= query_places[:, None]) & (key_places[None, :] >= 0)

def attend_grads(queries, grad_rows, key_window, value_window, allowed):
    query_rows = queries.shape[0]
    window = key_window.shape[0]
    kv_heads = key_window.shape[1] // HD
    group_size = queries.shape[1] // (kv_heads * HD)
    score_scale = 1.0 / math.sqrt(HD)
    q_four = queries.reshape(query_rows, kv_heads, group_size, HD).astype(jnp.float32)
    g_four = grad_rows.reshape(query_rows, kv_heads, group_size, HD).astype(jnp.float32)
    k_three = key_window.reshape(window, kv_heads, HD).astype(jnp.float32)
    v_three = value_window.reshape(window, kv_heads, HD).astype(jnp.float32)
    scores = jnp.einsum('bhgd,whd->hgbw', q_four, k_three) * score_scale
    scores = jnp.where(allowed, scores, -1e+30)
    row_max = lax.optimization_barrier(jnp.max(scores, axis=-1, keepdims=True))
    raised = jnp.exp(scores - row_max)
    prob_rows = raised / lax.optimization_barrier(jnp.sum(raised, axis=-1, keepdims=True))
    prob_half = prob_rows.astype(jnp.bfloat16).astype(jnp.float32)
    outputs = jnp.einsum('hgbw,whd->bhgd', prob_half, v_three)
    deltas = lax.optimization_barrier(jnp.sum(g_four * outputs, axis=-1))
    deltas = jnp.transpose(deltas, (1, 2, 0))[..., None]
    grad_prob = jnp.einsum('bhgd,whd->hgbw', g_four, v_three)
    grad_score = (prob_rows * (grad_prob - deltas)).astype(jnp.bfloat16).astype(jnp.float32)
    grad_query = (jnp.einsum('hgbw,whd->bhgd', grad_score, k_three) * score_scale).astype(jnp.bfloat16)
    grad_key = jnp.einsum('hgbw,bhgd->whd', grad_score, q_four) * score_scale
    grad_value = jnp.einsum('hgbw,bhgd->whd', prob_half, g_four)
    return (grad_query.reshape(query_rows, -1), grad_key, grad_value)

def reference(queries_first, queries_second, grads_first, grads_second, key_states, value_states, doc_lengths, hidden_states):
    padding = REACH * TOK_DEV
    window = (REACH + 1) * TOK_DEV
    kv_width = key_states.shape[1]
    stacked = jnp.concatenate([key_states, value_states], axis=1)
    stacked = jnp.concatenate([jnp.zeros((padding, stacked.shape[1]), stacked.dtype), stacked], axis=0)
    doc_ends = jnp.cumsum(doc_lengths).astype(jnp.int32)
    start_grads = jnp.zeros((SEQ + padding, 2 * kv_width), jnp.float32)

    def one_block(running, block_index):
        start = (block_index * TOK_DEV).astype(jnp.int32)
        window_rows = lax.dynamic_slice_in_dim(stacked, start, window, 0)
        key_window = window_rows[:, :kv_width]
        value_window = window_rows[:, kv_width:]
        query_places = start + jnp.arange(TOK_DEV, dtype=jnp.int32)
        key_places = start - padding + jnp.arange(window, dtype=jnp.int32)
        allowed = causal_mask(query_places, key_places, doc_ends)
        first_q, first_k, first_v = attend_grads(lax.dynamic_slice_in_dim(queries_first, start, TOK_DEV, 0), lax.dynamic_slice_in_dim(grads_first, start, TOK_DEV, 0), key_window, value_window, allowed)
        second_q, second_k, second_v = attend_grads(lax.dynamic_slice_in_dim(queries_second, start, TOK_DEV, 0), lax.dynamic_slice_in_dim(grads_second, start, TOK_DEV, 0), key_window, value_window, allowed)
        window_grads = jnp.stack([first_k + second_k, first_v + second_v], axis=2).reshape(window, -1)
        updated = lax.dynamic_slice_in_dim(running, start, window, 0) + window_grads
        running = lax.dynamic_update_slice_in_dim(running, updated, start, 0)
        return (running, (first_q, second_q))
    running, (all_first, all_second) = lax.scan(one_block, start_grads, jnp.arange(SEQ // TOK_DEV, dtype=jnp.int32))
    kv_grads = running[padding:].astype(jnp.bfloat16)
    weight_grad = jnp.dot(hidden_states.T, kv_grads, preferred_element_type=jnp.float32)
    return (all_first.reshape(SEQ, -1), all_second.reshape(SEQ, -1), weight_grad)
```

```python
import functools
import math

import jax
import jax.numpy as jnp
from jax import lax
from jax.experimental import pallas as pl
from jax.experimental.pallas import tpu as pltpu
from jax.sharding import PartitionSpec as P

HD = 128
REACH = 3
NT = (((1,), (1,)), ((), ()))


def attend_kernel(rows, group, here_ref, lens_ref, q1_ref, q2_ref, g1_ref, g2_ref, b3_ref, b2_ref, b1_ref, b0_ref,
                  dq1_ref, dq2_ref, f3_ref, f2_ref, f1_ref, own_ref, kv_ref, kt_ref, bias_ref, acc_ref):
    window = (REACH + 1) * rows
    half = rows // 2
    span = window - half
    scale = 1.0 / math.sqrt(HD)
    for i, ref in enumerate((b3_ref, b2_ref, b1_ref, b0_ref)):
        kv_ref[i * rows:(i + 1) * rows, :] = ref[...]
    kt_ref[...] = kv_ref[:, :HD].T
    base = here_ref[0] * rows
    places = base + lax.broadcasted_iota(jnp.int32, (1, rows), 1)

    def later(i, carry):
        end, first = carry
        end = end + lens_ref[i]
        return end, jnp.where(places >= end, end, first)

    _, first = lax.fori_loop(0, lens_ref.shape[0], later, (jnp.int32(0), jnp.zeros((1, rows), jnp.int32)))
    for side in range(2):
        keys = base - REACH * rows + side * half + lax.broadcasted_iota(jnp.int32, (span, half), 0)
        own = slice(side * half, (side + 1) * half)
        allowed = (keys >= first[:, own]) & (keys <= places[:, own])
        bias_ref[side] = jnp.where(allowed, 0.0, -1e30)
    acc_ref[...] = jnp.zeros_like(acc_ref)
    units = [(l, j) for l in range(2) for j in range(group)]
    for side in range(2):
        r = slice(side * half, (side + 1) * half)
        w = slice(side * half, side * half + span)
        k, v, kt = kv_ref[w, :HD], kv_ref[w, HD:], kt_ref[:, w]
        bias = bias_ref[side]
        bias2 = jnp.concatenate([bias, bias], axis=1)
        for n in range(0, len(units), 2):
            pair = units[n:n + 2]
            q = jnp.concatenate([(q1_ref, q2_ref)[l][r, j * HD:(j + 1) * HD] for l, j in pair], axis=0)
            g = jnp.concatenate([(g1_ref, g2_ref)[l][r, j * HD:(j + 1) * HD] for l, j in pair], axis=0)
            s = lax.dot_general(k, q, NT, preferred_element_type=jnp.float32) * (scale * math.log2(math.e)) + bias2
            dp = lax.dot_general(v, g, NT, preferred_element_type=jnp.float32)
            raised = jnp.exp2(s - jnp.max(s, axis=0, keepdims=True))
            p = raised * (1.0 / jnp.sum(raised, axis=0, keepdims=True))
            ph = p.astype(jnp.bfloat16)
            delta = jnp.sum(ph.astype(jnp.float32) * dp, axis=0, keepdims=True)
            ds = (p * (dp - delta)).astype(jnp.bfloat16)
            acc_ref[w, HD:] += jnp.dot(ph, g, preferred_element_type=jnp.float32)
            acc_ref[w, :HD] += jnp.dot(ds, q, preferred_element_type=jnp.float32)
            dqt = jnp.dot(kt, ds, preferred_element_type=jnp.float32) * scale
            dq = dqt.T.astype(jnp.bfloat16)
            for i, (l, j) in enumerate(pair):
                (dq1_ref, dq2_ref)[l][r, j * HD:(j + 1) * HD] = dq[i * half:(i + 1) * half]
    for i, ref in enumerate((f3_ref, f2_ref, f1_ref)):
        block = slice(i * rows, (i + 1) * rows)
        ref[:, :HD] = (acc_ref[block, :HD] * scale).astype(jnp.bfloat16)
        ref[:, HD:] = acc_ref[block, HD:].astype(jnp.bfloat16)
    own_ref[:, :HD] = acc_ref[REACH * rows:, :HD] * scale
    own_ref[:, HD:] = acc_ref[REACH * rows:, HD:]


def attend(c, kv_heads, here, lens, q1, q2, g1, g2, blocks):
    rows, width = q1.shape
    group = width // (kv_heads * HD)
    window = (REACH + 1) * rows
    cols = pl.BlockSpec((rows, group * HD), lambda i: (0, c))
    whole = lambda a: pl.BlockSpec(a.shape, lambda i: (0,) * a.ndim)
    smem = pl.BlockSpec(memory_space=pltpu.SMEM)
    flops = 5 * 2 * 2 * group * rows * window * HD
    return pl.pallas_call(
        functools.partial(attend_kernel, rows, group),
        grid=(1,),
        in_specs=[smem, smem, cols, cols, cols, cols] + [whole(b) for b in blocks],
        out_specs=[pl.BlockSpec((rows, group * HD), lambda i: (0, 0))] * 2
        + [pl.BlockSpec((rows, 2 * HD), lambda i: (0, 0))] * (REACH + 1),
        out_shape=[jax.ShapeDtypeStruct((rows, group * HD), jnp.bfloat16)] * 2
        + [jax.ShapeDtypeStruct((rows, 2 * HD), jnp.bfloat16)] * REACH + [jax.ShapeDtypeStruct((rows, 2 * HD), jnp.float32)],
        scratch_shapes=[pltpu.VMEM((window, 2 * HD), jnp.bfloat16), pltpu.VMEM((HD, window), jnp.bfloat16),
                        pltpu.VMEM((2, window - rows // 2, rows // 2), jnp.float32), pltpu.VMEM((window, 2 * HD), jnp.float32)],
        compiler_params=pltpu.CompilerParams(vmem_limit_bytes=48 * 1024 * 1024),
        cost_estimate=pl.CostEstimate(flops=flops, bytes_accessed=3 << 20, transcendentals=2 * group * rows * window),
        name="attend",
    )(here, lens, q1, q2, g1, g2, *blocks)


def moved(value, axis, place):
    pairs = [(i, place(i)) for i in range(lax.axis_size(axis))]
    return lax.ppermute(value, axis, [(i, j) for i, j in pairs if j is not None])


def project_kernel(picks_ref, hid_ref, *refs):
    blocks, (own_ref, away_ref) = refs[:-2], refs[-2:]
    total = None
    for j, block in enumerate(blocks):
        term = jnp.dot(hid_ref[picks_ref[j]], block[...], preferred_element_type=jnp.float32)
        total = term if total is None else total + term
    lanes, part = away_ref.shape[0] + 1, own_ref.shape[0]
    mine = picks_ref[len(blocks)]
    refs[-2][...] = jnp.zeros_like(own_ref)
    for d in range(lanes):
        piece = total[d * part:(d + 1) * part]

        @pl.when(mine == d)
        def _():
            own_ref[...] = piece

        for e in range(1, lanes):
            @pl.when((mine ^ e) == d)
            def _():
                away_ref[e - 1] = piece.astype(jnp.bfloat16)


def project(picks, hid, blocks, lanes):
    count, width, rows = hid.shape
    part = width // lanes
    columns = blocks[0].shape[1]
    vmem = pl.BlockSpec(memory_space=pltpu.VMEM)
    return pl.pallas_call(
        project_kernel,
        in_specs=[pl.BlockSpec(memory_space=pltpu.SMEM)] + [vmem] * (1 + count),
        out_specs=[vmem, vmem],
        out_shape=[jax.ShapeDtypeStruct((part, columns), jnp.float32),
                   jax.ShapeDtypeStruct((lanes - 1, part, columns), jnp.bfloat16)],
        compiler_params=pltpu.CompilerParams(vmem_limit_bytes=32 * 1024 * 1024),
        cost_estimate=pl.CostEstimate(flops=2 * count * width * rows * columns, bytes_accessed=4 << 20, transcendentals=0),
        name="project",
    )(picks, hid, *blocks)


def body(queries_first, queries_second, grads_first, grads_second, key_states, value_states, doc_lengths, hidden_states):
    rows = key_states.shape[0]
    kv_heads = key_states.shape[1] // HD
    tokens, heads = lax.axis_size("tok"), lax.axis_size("head")
    lanes = tokens // heads
    here, head = lax.axis_index("tok"), lax.axis_index("head")
    line, lane = here // lanes, here % lanes
    place = here.reshape(1).astype(jnp.int32)

    windows = []
    for c in range(kv_heads):
        own = jnp.concatenate([key_states[:, c * HD:(c + 1) * HD], value_states[:, c * HD:(c + 1) * HD]], axis=1)
        windows.append([moved(own, "tok", lambda t, s=s: t + s if t + s < tokens else None) for s in range(REACH, 0, -1)] + [own])

    def crossed(i):
        t, h = i // heads, i % heads
        return (h * lanes + t % lanes) * heads + t // lanes

    hid = moved(hidden_states.T[None], ("tok", "head"), crossed)
    step = heads // 2
    while step:
        hid = jnp.concatenate([hid, moved(hid, "head", lambda h: h ^ step)], axis=0)
        step //= 2
    order = [0]
    step = heads // 2
    while step:
        order = order + [i ^ step for i in order]
        step //= 2
    slot_of = jnp.asarray([order.index(i) for i in range(heads)], jnp.int32)
    picks = jnp.concatenate([slot_of[line ^ head ^ jnp.arange(heads)], lane.reshape(1)]).astype(jnp.int32)

    firsts, seconds, parts = [], [], []
    for c in range(kv_heads):
        first, second, *far, own = attend(
            c, kv_heads, place, doc_lengths, queries_first, queries_second, grads_first, grads_second, windows[c])
        firsts.append(first)
        seconds.append(second)
        total = own
        for s in range(1, REACH + 1):
            back = moved(far[REACH - s], "tok", lambda t, s=s: t - s if t >= s else None)
            total = total + back.astype(jnp.float32)
        kv_grads = total.astype(jnp.bfloat16)
        blocks = [kv_grads] + [
            moved(kv_grads, "tok", lambda t, j=j: ((t // lanes) ^ j) * lanes + t % lanes) for j in range(1, heads)]
        mine, away = project(picks, hid, blocks, lanes)
        for d in range(1, lanes):
            mine = mine + moved(away[d - 1], "tok", lambda t, d=d: t ^ d).astype(jnp.float32)
        parts.append(mine)
    return (jnp.concatenate(firsts, axis=1), jnp.concatenate(seconds, axis=1), jnp.concatenate(parts, axis=1))


def solution(mesh):
    split = P("tok", "head")
    return jax.shard_map(
        body,
        mesh=mesh,
        in_specs=(split,) * 6 + (P(), split),
        out_specs=(split,) * 3,
        check_vma=False,
    )
```

```python
import functools
import math

import jax
import jax.numpy as jnp
from jax import lax
from jax.experimental import pallas as pl
from jax.experimental.pallas import tpu as pltpu
from jax.sharding import PartitionSpec as P

HD = 128
REACH = 3
NT = (((1,), (1,)), ((), ()))


def attend(rows, group, shard, lens_ref, kv_ref, kt_ref, bias_ref, acc_ref, held_ref, made_ref, ready):
    window = (REACH + 1) * rows
    half = rows // 2
    span = window - half
    scale = 1.0 / math.sqrt(HD)
    kt_ref[...] = kv_ref[:, :HD].T
    base = shard * rows
    places = base + lax.broadcasted_iota(jnp.int32, (1, rows), 1)

    def later(i, carry):
        end, first = carry
        end = end + lens_ref[i]
        return end, jnp.where(places >= end, end, first)

    _, first = lax.fori_loop(0, lens_ref.shape[0], later, (jnp.int32(0), jnp.zeros((1, rows), jnp.int32)))
    for side in range(2):
        keys = base - REACH * rows + side * half + lax.broadcasted_iota(jnp.int32, (span, half), 0)
        own = slice(side * half, (side + 1) * half)
        allowed = (keys >= first[:, own]) & (keys <= places[:, own])
        bias_ref[side] = jnp.where(allowed, 0.0, -1e30)
    ready()
    units = [(l, j) for l in range(2) for j in range(group)]
    chunks = [units[n:n + 2] for n in range(0, len(units), 2)]
    steps = [(side, n) for side in range(2) for n in range(len(chunks))]

    def operands(side, n):
        r = slice(side * half, (side + 1) * half)
        q = jnp.concatenate([held_ref[l, r, j * HD:(j + 1) * HD] for l, j in chunks[n]], axis=0)
        g = jnp.concatenate([held_ref[2 + l, r, j * HD:(j + 1) * HD] for l, j in chunks[n]], axis=0)
        return q, g

    def products(side, n):
        w = slice(side * half, side * half + span)
        q, g = operands(side, n)
        s = lax.dot_general(kv_ref[w, :HD], q, NT, preferred_element_type=jnp.float32)
        dp = lax.dot_general(kv_ref[w, HD:], g, NT, preferred_element_type=jnp.float32)
        return s, dp

    ahead = products(*steps[0])
    for at, (side, n) in enumerate(steps):
        s, dp = ahead
        if at + 1 < len(steps):
            ahead = products(*steps[at + 1])
        w = slice(side * half, side * half + span)
        r = slice(side * half, (side + 1) * half)
        bias = bias_ref[side]
        s = s * (scale * math.log2(math.e)) + jnp.concatenate([bias] * len(chunks[n]), axis=1)
        raised = jnp.exp2(s - jnp.max(s, axis=0, keepdims=True))
        p = raised * (1.0 / jnp.sum(raised, axis=0, keepdims=True))
        ph = p.astype(jnp.bfloat16)
        delta = jnp.sum(ph.astype(jnp.float32) * dp, axis=0, keepdims=True)
        ds = (p * (dp - delta)).astype(jnp.bfloat16)
        q, g = operands(side, n)
        if side == 0 and n == 0:
            acc_ref[span:, :] = jnp.zeros((half, 2 * HD), jnp.float32)
            acc_ref[w, HD:] = jnp.dot(ph, g, preferred_element_type=jnp.float32)
            acc_ref[w, :HD] = jnp.dot(ds, q, preferred_element_type=jnp.float32)
        else:
            acc_ref[w, HD:] += jnp.dot(ph, g, preferred_element_type=jnp.float32)
            acc_ref[w, :HD] += jnp.dot(ds, q, preferred_element_type=jnp.float32)
        dq = (jnp.dot(kt_ref[:, w], ds, preferred_element_type=jnp.float32) * scale).T.astype(jnp.bfloat16)
        for i, (l, j) in enumerate(chunks[n]):
            made_ref[l, r, j * HD:(j + 1) * HD] = dq[i * half:(i + 1) * half]


def attend_scratch(rows):
    keys = (REACH + 1) * rows
    return [pltpu.VMEM((keys, 2 * HD), jnp.bfloat16), pltpu.VMEM((HD, keys), jnp.bfloat16),
            pltpu.VMEM((2, keys - rows // 2, rows // 2), jnp.float32)]


def chosen(lane, kv_ref, i, ref, other):
    rows = ref.shape[0]
    if ref is other:
        kv_ref[i * rows:(i + 1) * rows, :] = ref[...]
        return

    @pl.when(lane == 0)
    def _():
        kv_ref[i * rows:(i + 1) * rows, :] = ref[...]

    @pl.when(lane == 1)
    def _():
        kv_ref[i * rows:(i + 1) * rows, :] = other[...]


def fetched(arrays, columns, held_ref, sems):
    copies = [pltpu.make_async_copy(ref.at[:, columns], held_ref.at[i], sems.at[i]) for i, ref in enumerate(arrays)]
    for copy in copies:
        copy.start()

    def ready():
        for copy in copies:
            copy.wait()

    return ready


def scaled(term):
    return jnp.concatenate([term[:, :HD] * (1.0 / math.sqrt(HD)), term[:, HD:]], axis=1)


def whole_kernel(head, rows, group, here_ref, lens_ref, q1, q2, g1, g2, b3, b2, b1, b0,
                 made_ref, f3_ref, f2_ref, f1_ref, own_ref, kv_ref, kt_ref, bias_ref, acc_ref, held_ref, sems):
    ready = fetched((q1, q2, g1, g2), slice(head * group * HD, (head + 1) * group * HD), held_ref, sems)
    for i, ref in enumerate((b3, b2, b1, b0)):
        kv_ref[i * rows:(i + 1) * rows, :] = ref[...]
    attend(rows, group, here_ref[0], lens_ref, kv_ref, kt_ref, bias_ref, acc_ref, held_ref, made_ref, ready)
    for i, ref in enumerate((f3_ref, f2_ref, f1_ref, own_ref)):
        ref[...] = scaled(acc_ref[i * rows:(i + 1) * rows, :]).astype(ref.dtype)


def first_kernel(rows, group, here_ref, lens_ref, q1, q2, g1, g2, far, lifted, mine, got,
                 made_ref, acc_ref, kv_ref, kt_ref, bias_ref, held_ref, sems):
    lane = here_ref[0] % 2
    ready = fetched((q1, q2, g1, g2), pl.ds(pl.multiple_of(lane * group * HD, HD), group * HD), held_ref, sems)
    along, crosswise = lifted.at[0], lifted.at[1]
    for i, pair in enumerate(((far, crosswise), (along, along), (crosswise, got), (mine, mine))):
        chosen(lane, kv_ref, i, *pair)
    attend(rows, group, here_ref[0], lens_ref, kv_ref, kt_ref, bias_ref, acc_ref, held_ref, made_ref, ready)


def second_kernel(rows, group, here_ref, lens_ref, held_ref, far, lifted, mine, got, before_ref,
                  made_ref, far_ref, pair_ref, own_ref, kv_ref, kt_ref, bias_ref, acc_ref):
    lane = here_ref[0] % 2
    along, crosswise = lifted.at[0], lifted.at[1]
    for i, pair in enumerate(((along, far), (crosswise, crosswise), (mine, along), (got, got))):
        chosen(lane, kv_ref, i, *pair)
    attend(rows, group, here_ref[0] + 1 - 2 * lane, lens_ref, kv_ref, kt_ref, bias_ref, acc_ref, held_ref, made_ref, lambda: None)

    def merged(even_ref, odd_ref):
        block = lambda ref, i: ref[i * rows:(i + 1) * rows, :]
        far_ref[...] = scaled(block(even_ref, 0)).astype(far_ref.dtype)
        for i in range(2):
            pair_ref[i] = scaled(block(even_ref, 1 + i) + block(odd_ref, i)).astype(pair_ref.dtype)
        own_ref[0] = scaled(block(even_ref, 3) + block(odd_ref, 2))
        own_ref[1] = scaled(block(odd_ref, 3))

    @pl.when(lane == 0)
    def _():
        merged(before_ref, acc_ref)

    @pl.when(lane == 1)
    def _():
        merged(acc_ref, before_ref)


def called(kernel, name, operands, kinds, outs, scratch):
    places = {"s": pltpu.SMEM, "v": pltpu.VMEM, "h": pltpu.HBM}
    return pl.pallas_call(
        kernel,
        in_specs=[pl.BlockSpec(memory_space=places[k]) for k in kinds],
        out_specs=[pl.BlockSpec(memory_space=pltpu.VMEM)] * len(outs),
        out_shape=[jax.ShapeDtypeStruct(shape, dtype) for shape, dtype in outs],
        scratch_shapes=scratch,
        compiler_params=pltpu.CompilerParams(vmem_limit_bytes=44 * 1024 * 1024),
        cost_estimate=pl.CostEstimate(flops=1 << 15, bytes_accessed=1 << 15, transcendentals=0),
        name=name,
    )(*operands)


def moved(value, axis, place):
    pairs = [(i, place(i)) for i in range(lax.axis_size(axis))]
    return lax.ppermute(value, axis, [(i, j) for i, j in pairs if j is not None])


def after(value, *earlier):
    return lax.optimization_barrier((value,) + earlier)[0]


def gathered(kv_grads, heads, lanes):
    return [kv_grads] + [
        moved(kv_grads, "tok", lambda t, j=j: ((t // lanes) ^ j) * lanes + t % lanes) for j in range(1, heads)]


def project_kernel(count, paired, picks_ref, *refs):
    blocks, hids, (own_ref, away_ref) = refs[:count], refs[count:-2], refs[-2:]
    line, head, mine = picks_ref[0], picks_ref[1], picks_ref[2]
    total = None
    for j, block in enumerate(blocks):
        if paired:
            near = (line ^ j) % 2 == head % 2
            y = head // 2
            terms = []
            for e in range(2):
                slots = [4 * e + 2 * (y ^ q) + j // 2 for q in range(2)]
                pieces = [jnp.where(near, hids[0][slot], hids[1][slot]) for slot in slots]
                terms.append((jnp.concatenate(pieces, axis=1), block[mine ^ e]))
        else:
            slot, step = 0, 1
            while step < count:
                slot = 2 * slot + ((line ^ j ^ head) // step) % 2
                step *= 2
            terms = [(hids[0][slot], block[...])]
        for turned, grads in terms:
            term = jnp.dot(turned, grads, preferred_element_type=jnp.float32)
            total = term if total is None else total + term
    lanes, part = away_ref.shape[0] + 1, own_ref.shape[0]
    own_ref[...] = jnp.zeros_like(own_ref)
    for d in range(lanes):
        piece = total[d * part:(d + 1) * part]

        @pl.when(mine == d)
        def _():
            own_ref[...] = piece

        for e in range(1, lanes):
            @pl.when((mine ^ e) == d)
            def _():
                away_ref[e - 1] = piece.astype(jnp.bfloat16)


def project(picks, hids, blocks, lanes):
    part = hids[0].shape[-2] // lanes
    columns = blocks[0].shape[-1]
    return called(
        functools.partial(project_kernel, len(blocks), len(hids) > 1), "project", [picks, *blocks, *hids],
        "s" + "v" * (len(blocks) + len(hids)),
        [((part, columns), jnp.float32), ((lanes - 1, part, columns), jnp.bfloat16)], [])


def general(place, line, lane, head, heads, tokens, lanes, kv_heads, lens, arrays, stacked, hidden_states):
    def crossed(i):
        t, h = i // heads, i % heads
        return (h * lanes + t % lanes) * heads + t // lanes

    hid = moved(hidden_states.T[None], ("tok", "head"), crossed)
    step = heads // 2
    while step:
        hid = jnp.concatenate([hid, moved(hid, "head", lambda h: h ^ step)], axis=0)
        step //= 2
    picks = jnp.stack([line, head, lane]).astype(jnp.int32)
    rows, width = arrays[0].shape
    group = width // (kv_heads * HD)
    block = (rows, 2 * HD)
    firsts, seconds, parts = [], [], []
    for c, own in enumerate(stacked):
        window = [moved(own, "tok", lambda t, s=s: t + s if t + s < tokens else None) for s in range(REACH, 0, -1)] + [own]
        made, *far, total = called(
            functools.partial(whole_kernel, c, rows, group), "attend", [place, lens, *arrays, *window],
            "ss" + "h" * 4 + "v" * 4,
            [((2, rows, group * HD), jnp.bfloat16)] + [(block, jnp.bfloat16)] * REACH + [(block, jnp.float32)],
            attend_scratch(rows) + [pltpu.VMEM(((REACH + 1) * rows, 2 * HD), jnp.float32),
                                    pltpu.VMEM((4, rows, group * HD), jnp.bfloat16), pltpu.SemaphoreType.DMA((4,))])
        firsts.append(made[0])
        seconds.append(made[1])
        for s in range(1, REACH + 1):
            back = moved(far[REACH - s], "tok", lambda t, s=s: t - s if t >= s else None)
            total = total + back.astype(jnp.float32)
        mine, away = project(picks, [hid], gathered(total.astype(jnp.bfloat16), heads, lanes), lanes)
        for d in range(1, lanes):
            mine = mine + moved(away[d - 1], "tok", lambda t, d=d: t ^ d).astype(jnp.float32)
        parts.append(mine)
    return tuple(jnp.concatenate(x, axis=1) for x in (firsts, seconds, parts))


def paired(place, line, lane, head, heads, tokens, lanes, kv_heads, lens, arrays, stacked, hidden_states):
    both = ("tok", "head")
    rows, width = arrays[0].shape
    group = width // (kv_heads * HD)
    wide = group * HD
    even = lane == 0

    def mine_and_other(a, b):
        return jnp.where(even, a, b), jnp.where(even, b, a)

    def up(value, lines):
        return moved(value, "tok", lambda t: t + lines * lanes if t + lines * lanes < tokens else None)

    def down(value, lines):
        return moved(value, "tok", lambda t: t - lines * lanes if t >= lines * lanes else None)

    def over(value):
        return moved(value, "tok", lambda t: t ^ 1)

    def crossed(flip):
        def place_of(i):
            t, h = i // heads, i % heads
            z, c = t // lanes, h % 2
            return (((z // 2) ^ flip) * 2 + c) * lanes * heads + (t % lanes) * heads + (h // 2) * 2 + z % 2
        return place_of

    given = jnp.where(even, stacked[1], stacked[0])
    mine = jnp.where(even, after(stacked[0], given), stacked[1])
    got = over(given)
    risen = jnp.stack([mine, got])
    lifted = up(risen, 1)
    far = up(jnp.where(even, got, mine), 2)
    asked = over(jnp.stack([jnp.where(even, a[:, wide:], a[:, :wide]) for a in (after(x, given) for x in arrays)]))
    y = head // 2
    half = rows // 2
    kept, lent = (lax.dynamic_slice_in_dim(hidden_states, at * half, half, 0) for at in (y, 1 - y))
    lent = moved(lent, "head", lambda h: h ^ 2)
    own_line = (line // 2) == y
    afar = moved(after(jnp.where(own_line, lent, kept), lifted, far), both, crossed(1))

    window = [far, lifted, mine, got]
    keys = (REACH + 1) * rows
    made, sums = called(
        functools.partial(first_kernel, rows, group), "attend_own", [place, lens, *arrays, *window], "ss" + "h" * 4 + "v" * 4,
        [((2, rows, wide), jnp.bfloat16), ((keys, 2 * HD), jnp.float32)],
        attend_scratch(rows) + [pltpu.VMEM((4, rows, wide), jnp.bfloat16), pltpu.SemaphoreType.DMA((4,))])
    nearby = moved(after(jnp.where(own_line, kept, lent), sums), both, crossed(0))
    made_other, farther, nearer, own = called(
        functools.partial(second_kernel, rows, group), "attend_other", [place, lens, asked, *window, after(sums, afar)],
        "ss" + "v" * 6,
        [((2, rows, wide), jnp.bfloat16), ((rows, 2 * HD), jnp.bfloat16), ((2, rows, 2 * HD), jnp.bfloat16),
         ((2, rows, 2 * HD), jnp.float32)],
        attend_scratch(rows) + [pltpu.VMEM((keys, 2 * HD), jnp.float32)])

    one, two = down(nearer, 1), down(farther, 2)
    hops = jnp.swapaxes(jnp.stack([nearby, after(afar, own)]), 1, 2)
    beside = over(hops)
    hids = [hops, moved(hops, "head", lambda h: h ^ 2), beside, moved(beside, "head", lambda h: h ^ 2)]
    total = (own + one.astype(jnp.float32)).at[1].add(two.astype(jnp.float32)).astype(jnp.bfloat16)
    across = moved(total, "tok", lambda t: t ^ (2 * lanes))
    blocks = [total, moved(total, "tok", lambda t: t ^ lanes), across, moved(across, "tok", lambda t: t ^ lanes)]
    sent = over(after(made_other, total))
    hids = jnp.concatenate([after(hids[0], *blocks[1:3])] + hids[1:], axis=0)
    firsts, seconds = (jnp.concatenate(mine_and_other(after(made[l], hids), sent[l]), axis=1) for l in range(2))

    picks = jnp.stack([line, head, lane]).astype(jnp.int32)
    kept, away = project(picks, [hids, moved(hids, "head", lambda h: h ^ 1)], blocks, lanes)
    came = over(away[0]).astype(jnp.float32)
    return (firsts, seconds, jnp.concatenate(mine_and_other(kept, came), axis=1))


def body(queries_first, queries_second, grads_first, grads_second, key_states, value_states, doc_lengths, hidden_states):
    kv_heads = key_states.shape[1] // HD
    tokens, heads = lax.axis_size("tok"), lax.axis_size("head")
    lanes = tokens // heads
    here, head = lax.axis_index("tok"), lax.axis_index("head")
    arrays = (queries_first, queries_second, grads_first, grads_second)
    stacked = [jnp.concatenate([key_states[:, c * HD:(c + 1) * HD], value_states[:, c * HD:(c + 1) * HD]], axis=1)
               for c in range(kv_heads)]
    plan = paired if (lanes, heads, kv_heads, REACH) == (2, 4, 2, 3) else general
    return plan(here.reshape(1).astype(jnp.int32), here // lanes, here % lanes, head, heads, tokens, lanes, kv_heads,
                doc_lengths, arrays, stacked, hidden_states)


def solution(mesh):
    split = P("tok", "head")
    return jax.shard_map(
        body,
        mesh=mesh,
        in_specs=(split,) * 6 + (P(), split),
        out_specs=(split,) * 3,
        check_vma=False,
    )
```

```python
import functools
import math

import jax
import jax.numpy as jnp
from jax import lax
from jax.experimental import pallas as pl
from jax.experimental.pallas import tpu as pltpu
from jax.sharding import PartitionSpec as P

HD = 128
REACH = 3
NT = (((1,), (1,)), ((), ()))


def attend(rows, group, shard, lens_ref, kv_ref, kt_ref, bias_ref, acc_ref, held_ref, made_ref, ready):
    window = (REACH + 1) * rows
    half = rows // 2
    span = window - half
    scale = 1.0 / math.sqrt(HD)
    kt_ref[...] = kv_ref[:, :HD].T
    base = shard * rows
    places = base + lax.broadcasted_iota(jnp.int32, (1, rows), 1)

    def later(i, carry):
        end, first = carry
        end = end + lens_ref[i]
        return end, jnp.where(places >= end, end, first)

    _, first = lax.fori_loop(0, lens_ref.shape[0], later, (jnp.int32(0), jnp.zeros((1, rows), jnp.int32)))
    for side in range(2):
        keys = base - REACH * rows + side * half + lax.broadcasted_iota(jnp.int32, (span, half), 0)
        own = slice(side * half, (side + 1) * half)
        allowed = (keys >= first[:, own]) & (keys <= places[:, own])
        bias_ref[side] = jnp.where(allowed, 0.0, -1e30)
    ready()
    units = [(l, j) for l in range(2) for j in range(group)]
    chunks = [units[n:n + 2] for n in range(0, len(units), 2)]
    steps = [(side, n) for side in range(2) for n in range(len(chunks))]

    def operands(side, n):
        r = slice(side * half, (side + 1) * half)
        q = jnp.concatenate([held_ref[l, r, j * HD:(j + 1) * HD] for l, j in chunks[n]], axis=0)
        g = jnp.concatenate([held_ref[2 + l, r, j * HD:(j + 1) * HD] for l, j in chunks[n]], axis=0)
        return q, g

    def products(side, n):
        w = slice(side * half, side * half + span)
        q, g = operands(side, n)
        s = lax.dot_general(kv_ref[w, :HD], q, NT, preferred_element_type=jnp.float32)
        dp = lax.dot_general(kv_ref[w, HD:], g, NT, preferred_element_type=jnp.float32)
        return s, dp

    ahead = products(*steps[0])
    for at, (side, n) in enumerate(steps):
        s, dp = ahead
        if at + 1 < len(steps):
            ahead = products(*steps[at + 1])
        w = slice(side * half, side * half + span)
        r = slice(side * half, (side + 1) * half)
        bias = bias_ref[side]
        s = s * (scale * math.log2(math.e)) + jnp.concatenate([bias] * len(chunks[n]), axis=1)
        raised = jnp.exp2(s - jnp.max(s, axis=0, keepdims=True))
        p = raised * (1.0 / jnp.sum(raised, axis=0, keepdims=True))
        ph = p.astype(jnp.bfloat16)
        delta = jnp.sum(ph.astype(jnp.float32) * dp, axis=0, keepdims=True)
        ds = (p * (dp - delta)).astype(jnp.bfloat16)
        q, g = operands(side, n)
        if side == 0 and n == 0:
            acc_ref[span:, :] = jnp.zeros((half, 2 * HD), jnp.float32)
            acc_ref[w, HD:] = jnp.dot(ph, g, preferred_element_type=jnp.float32)
            acc_ref[w, :HD] = jnp.dot(ds, q, preferred_element_type=jnp.float32)
        else:
            acc_ref[w, HD:] += jnp.dot(ph, g, preferred_element_type=jnp.float32)
            acc_ref[w, :HD] += jnp.dot(ds, q, preferred_element_type=jnp.float32)
        dq = (jnp.dot(kt_ref[:, w], ds, preferred_element_type=jnp.float32) * scale).T.astype(jnp.bfloat16)
        for i, (l, j) in enumerate(chunks[n]):
            made_ref[l, r, j * HD:(j + 1) * HD] = dq[i * half:(i + 1) * half]


def attend_scratch(rows):
    keys = (REACH + 1) * rows
    return [pltpu.VMEM((keys, 2 * HD), jnp.bfloat16), pltpu.VMEM((HD, keys), jnp.bfloat16),
            pltpu.VMEM((2, keys - rows // 2, rows // 2), jnp.float32)]


def chosen(lane, kv_ref, i, ref, other):
    rows = ref.shape[0]
    if ref is other:
        kv_ref[i * rows:(i + 1) * rows, :] = ref[...]
        return

    @pl.when(lane == 0)
    def _():
        kv_ref[i * rows:(i + 1) * rows, :] = ref[...]

    @pl.when(lane == 1)
    def _():
        kv_ref[i * rows:(i + 1) * rows, :] = other[...]


def fetched(arrays, columns, held_ref, sems):
    copies = [pltpu.make_async_copy(ref.at[:, columns], held_ref.at[i], sems.at[i]) for i, ref in enumerate(arrays)]
    for copy in copies:
        copy.start()

    def ready():
        for copy in copies:
            copy.wait()

    return ready


def scaled(term):
    return jnp.concatenate([term[:, :HD] * (1.0 / math.sqrt(HD)), term[:, HD:]], axis=1)


def whole_kernel(head, rows, group, here_ref, lens_ref, q1, q2, g1, g2, b3, b2, b1, b0,
                 made_ref, f3_ref, f2_ref, f1_ref, own_ref, kv_ref, kt_ref, bias_ref, acc_ref, held_ref, sems):
    ready = fetched((q1, q2, g1, g2), slice(head * group * HD, (head + 1) * group * HD), held_ref, sems)
    for i, ref in enumerate((b3, b2, b1, b0)):
        kv_ref[i * rows:(i + 1) * rows, :] = ref[...]
    attend(rows, group, here_ref[0], lens_ref, kv_ref, kt_ref, bias_ref, acc_ref, held_ref, made_ref, ready)
    for i, ref in enumerate((f3_ref, f2_ref, f1_ref, own_ref)):
        ref[...] = scaled(acc_ref[i * rows:(i + 1) * rows, :]).astype(ref.dtype)


def called(kernel, name, operands, kinds, outs, scratch, mebibytes=44):
    places = {"s": pltpu.SMEM, "v": pltpu.VMEM, "h": pltpu.HBM, "a": pl.ANY}
    return pl.pallas_call(
        kernel,
        in_specs=[pl.BlockSpec(memory_space=places[k]) for k in kinds],
        out_specs=[pl.BlockSpec(memory_space=pltpu.VMEM)] * len(outs),
        out_shape=[jax.ShapeDtypeStruct(shape, dtype) for shape, dtype in outs],
        scratch_shapes=scratch,
        compiler_params=pltpu.CompilerParams(vmem_limit_bytes=mebibytes * 1024 * 1024),
        cost_estimate=pl.CostEstimate(flops=1 << 15, bytes_accessed=1 << 15, transcendentals=0),
        name=name,
    )(*operands)


def moved(value, axis, place):
    pairs = [(i, place(i)) for i in range(lax.axis_size(axis))]
    return lax.ppermute(value, axis, [(i, j) for i, j in pairs if j is not None])


def after(value, *earlier):
    return lax.optimization_barrier((value,) + earlier)[0]


def gathered(kv_grads, heads, lanes):
    return [kv_grads] + [
        moved(kv_grads, "tok", lambda t, j=j: ((t // lanes) ^ j) * lanes + t % lanes) for j in range(1, heads)]


def project_kernel(count, paired, picks_ref, *refs):
    blocks, hids, (own_ref, away_ref) = refs[:count], refs[count:-2], refs[-2:]
    line, head, mine = picks_ref[0], picks_ref[1], picks_ref[2]
    total = None
    for j, block in enumerate(blocks):
        if paired:
            near = (line ^ j) % 2 == head % 2
            y = head // 2
            terms = []
            for e in range(2):
                slots = [4 * e + 2 * (y ^ q) + j // 2 for q in range(2)]
                pieces = [jnp.where(near, hids[0][slot], hids[1][slot]) for slot in slots]
                terms.append((jnp.concatenate(pieces, axis=1), block[mine ^ e]))
        else:
            slot, step = 0, 1
            while step < count:
                slot = 2 * slot + ((line ^ j ^ head) // step) % 2
                step *= 2
            terms = [(hids[0][slot], block[...])]
        for turned, grads in terms:
            term = jnp.dot(turned, grads, preferred_element_type=jnp.float32)
            total = term if total is None else total + term
    lanes, part = away_ref.shape[0] + 1, own_ref.shape[0]
    own_ref[...] = jnp.zeros_like(own_ref)
    for d in range(lanes):
        piece = total[d * part:(d + 1) * part]

        @pl.when(mine == d)
        def _():
            own_ref[...] = piece

        for e in range(1, lanes):
            @pl.when((mine ^ e) == d)
            def _():
                away_ref[e - 1] = piece.astype(jnp.bfloat16)


def project(picks, hids, blocks, lanes):
    part = hids[0].shape[-2] // lanes
    columns = blocks[0].shape[-1]
    return called(
        functools.partial(project_kernel, len(blocks), len(hids) > 1), "project", [picks, *blocks, *hids],
        "s" + "v" * (len(blocks) + len(hids)),
        [((part, columns), jnp.float32), ((lanes - 1, part, columns), jnp.bfloat16)], [])


def first_kernel(rows, group, here_ref, lens_ref, q1, q2, g1, g2, far, lifted, mine, got,
                 made_ref, acc_ref, kv_ref, kt_ref, bias_ref, held_ref, sems):
    lane = here_ref[0] % 2
    ready = fetched((q1, q2, g1, g2), pl.ds(pl.multiple_of(lane * group * HD, HD), group * HD), held_ref, sems)
    along, crosswise = lifted.at[0], lifted.at[1]
    for i, pair in enumerate(((far, crosswise), (along, along), (crosswise, got), (mine, mine))):
        chosen(lane, kv_ref, i, *pair)
    attend(rows, group, here_ref[0], lens_ref, kv_ref, kt_ref, bias_ref, acc_ref, held_ref, made_ref, ready)


def second_kernel(rows, group, here_ref, lens_ref, held_ref, far, lifted, mine, got, before_ref,
                  made_ref, far_ref, pair_ref, own_ref, kv_ref, kt_ref, bias_ref, acc_ref):
    lane = here_ref[0] % 2
    along, crosswise = lifted.at[0], lifted.at[1]
    for i, pair in enumerate(((along, far), (crosswise, crosswise), (mine, along), (got, got))):
        chosen(lane, kv_ref, i, *pair)
    attend(rows, group, here_ref[0] + 1 - 2 * lane, lens_ref, kv_ref, kt_ref, bias_ref, acc_ref, held_ref, made_ref, lambda: None)

    def merged(even_ref, odd_ref):
        block = lambda ref, i: ref[i * rows:(i + 1) * rows, :]
        far_ref[...] = scaled(block(even_ref, 0)).astype(far_ref.dtype)
        for i in range(2):
            pair_ref[i] = scaled(block(even_ref, 1 + i) + block(odd_ref, i)).astype(pair_ref.dtype)
        own_ref[0] = scaled(block(even_ref, 3) + block(odd_ref, 2))
        own_ref[1] = scaled(block(odd_ref, 3))

    @pl.when(lane == 0)
    def _():
        merged(before_ref, acc_ref)

    @pl.when(lane == 1)
    def _():
        merged(acc_ref, before_ref)


def general(place, line, lane, head, heads, tokens, lanes, kv_heads, lens, arrays, stacked, hidden_states):
    def crossed(i):
        t, h = i // heads, i % heads
        return (h * lanes + t % lanes) * heads + t // lanes

    hid = moved(hidden_states.T[None], ("tok", "head"), crossed)
    step = heads // 2
    while step:
        hid = jnp.concatenate([hid, moved(hid, "head", lambda h: h ^ step)], axis=0)
        step //= 2
    picks = jnp.stack([line, head, lane]).astype(jnp.int32)
    rows, width = arrays[0].shape
    group = width // (kv_heads * HD)
    block = (rows, 2 * HD)
    firsts, seconds, parts = [], [], []
    for c, own in enumerate(stacked):
        window = [moved(own, "tok", lambda t, s=s: t + s if t + s < tokens else None) for s in range(REACH, 0, -1)] + [own]
        made, *far, total = called(
            functools.partial(whole_kernel, c, rows, group), "attend", [place, lens, *arrays, *window],
            "ss" + "h" * 4 + "v" * 4,
            [((2, rows, group * HD), jnp.bfloat16)] + [(block, jnp.bfloat16)] * REACH + [(block, jnp.float32)],
            attend_scratch(rows) + [pltpu.VMEM(((REACH + 1) * rows, 2 * HD), jnp.float32),
                                    pltpu.VMEM((4, rows, group * HD), jnp.bfloat16), pltpu.SemaphoreType.DMA((4,))])
        firsts.append(made[0])
        seconds.append(made[1])
        for s in range(1, REACH + 1):
            back = moved(far[REACH - s], "tok", lambda t, s=s: t - s if t >= s else None)
            total = total + back.astype(jnp.float32)
        mine, away = project(picks, [hid], gathered(total.astype(jnp.bfloat16), heads, lanes), lanes)
        for d in range(1, lanes):
            mine = mine + moved(away[d - 1], "tok", lambda t, d=d: t ^ d).astype(jnp.float32)
        parts.append(mine)
    return tuple(jnp.concatenate(x, axis=1) for x in (firsts, seconds, parts))


def paired(place, line, lane, head, heads, tokens, lanes, kv_heads, lens, arrays, stacked, hidden_states):
    both = ("tok", "head")
    rows, width = arrays[0].shape
    group = width // (kv_heads * HD)
    wide = group * HD
    even = lane == 0

    def mine_and_other(a, b):
        return jnp.where(even, a, b), jnp.where(even, b, a)

    def up(value, lines):
        return moved(value, "tok", lambda t: t + lines * lanes if t + lines * lanes < tokens else None)

    def down(value, lines):
        return moved(value, "tok", lambda t: t - lines * lanes if t >= lines * lanes else None)

    def over(value):
        return moved(value, "tok", lambda t: t ^ 1)

    def crossed(flip):
        def place_of(i):
            t, h = i // heads, i % heads
            z, c = t // lanes, h % 2
            return (((z // 2) ^ flip) * 2 + c) * lanes * heads + (t % lanes) * heads + (h // 2) * 2 + z % 2
        return place_of

    y = head // 2
    half = rows // 2
    given = jnp.where(even, stacked[1], stacked[0])
    mine = jnp.where(even, after(stacked[0], given), stacked[1])
    got = over(given)
    asked = over(jnp.stack([jnp.where(even, a[:, wide:], a[:, :wide]) for a in (after(x, given) for x in arrays)]))
    risen = jnp.stack([mine, got])
    lifted = up(risen, 1)
    far = up(jnp.where(even, got, mine), 2)
    kept, lent = (lax.dynamic_slice_in_dim(after(hidden_states, given), at * half, half, 0) for at in (y, 1 - y))
    lent = moved(lent, "head", lambda h: h ^ 2)
    own_line = (line // 2) == y
    afar = moved(after(jnp.where(own_line, lent, kept), lifted, far), both, crossed(1))
    window = [far, lifted, mine, got]
    keys = (REACH + 1) * rows
    made, sums = called(
        functools.partial(first_kernel, rows, group), "attend_own", [place, lens, *arrays, *window], "ss" + "h" * 4 + "v" * 4,
        [((2, rows, wide), jnp.bfloat16), ((keys, 2 * HD), jnp.float32)],
        attend_scratch(rows) + [pltpu.VMEM((4, rows, wide), jnp.bfloat16), pltpu.SemaphoreType.DMA((4,))])
    nearby = moved(after(jnp.where(own_line, kept, lent), sums), both, crossed(0))
    made_other, farther, nearer, own = called(
        functools.partial(second_kernel, rows, group), "attend_other", [place, lens, asked, *window, after(sums, afar)],
        "ss" + "v" * 6,
        [((2, rows, wide), jnp.bfloat16), ((rows, 2 * HD), jnp.bfloat16), ((2, rows, 2 * HD), jnp.bfloat16),
         ((2, rows, 2 * HD), jnp.float32)],
        attend_scratch(rows) + [pltpu.VMEM((keys, 2 * HD), jnp.float32)])
    one, two = down(nearer, 1), down(farther, 2)
    sent = over(made_other)
    hops = jnp.swapaxes(jnp.stack([nearby, after(afar, own)]), 1, 2)
    beside, upright = over(hops), moved(hops, "head", lambda h: h ^ 2)
    skew = moved(after(beside, one), "head", lambda h: h ^ 2)
    total = (own + one.astype(jnp.float32)).at[1].add(two.astype(jnp.float32)).astype(jnp.bfloat16)
    across = moved(total, "tok", lambda t: t ^ (2 * lanes))
    j1 = moved(total, "tok", lambda t: t ^ lanes)
    blocks = [total, j1, across, moved(after(across, j1), "tok", lambda t: t ^ lanes)]
    hids = jnp.concatenate([after(hops, j1, across, sent), upright, beside, skew], axis=0)
    picks = jnp.stack([line, head, lane]).astype(jnp.int32)
    kept, away = project(picks, [hids, moved(hids, "head", lambda h: h ^ 1)], blocks, lanes)
    came = over(away[0]).astype(jnp.float32)
    firsts, seconds = (jnp.concatenate(mine_and_other(made[l], sent[l]), axis=1) for l in range(2))
    return (firsts, seconds, jnp.concatenate(mine_and_other(kept, came), axis=1))


def body(queries_first, queries_second, grads_first, grads_second, key_states, value_states, doc_lengths, hidden_states):
    kv_heads = key_states.shape[1] // HD
    tokens, heads = lax.axis_size("tok"), lax.axis_size("head")
    lanes = tokens // heads
    here, head = lax.axis_index("tok"), lax.axis_index("head")
    arrays = (queries_first, queries_second, grads_first, grads_second)
    stacked = [jnp.concatenate([x[:, c * HD:(c + 1) * HD] for x in (key_states, value_states)], axis=1) for c in range(kv_heads)]
    plan = paired if (lanes, heads, kv_heads, REACH) == (2, 4, 2, 3) else general
    return plan(here.reshape(1).astype(jnp.int32), here // lanes, here % lanes, head, heads, tokens, lanes, kv_heads,
                doc_lengths, arrays, stacked, hidden_states)


def solution(mesh):
    split = P("tok", "head")
    return jax.shard_map(
        body,
        mesh=mesh,
        in_specs=(split,) * 6 + (P(), split),
        out_specs=(split,) * 3,
        check_vma=False,
    )
```

```python
import functools
import math

import jax
import jax.numpy as jnp
from jax import lax
from jax.experimental import pallas as pl
from jax.experimental.pallas import tpu as pltpu
from jax.sharding import PartitionSpec as P

HD = 128
REACH = 3
NT = (((1,), (1,)), ((), ()))


def attend(rows, group, shard, lens_ref, kv_ref, kt_ref, bias_ref, acc_ref, held_ref, made_ref, ready):
    window = (REACH + 1) * rows
    half = rows // 2
    span = window - half
    scale = 1.0 / math.sqrt(HD)
    kt_ref[...] = kv_ref[:, :HD].T
    base = shard * rows
    places = base + lax.broadcasted_iota(jnp.int32, (1, rows), 1)

    def later(i, carry):
        end, first = carry
        end = end + lens_ref[i]
        return end, jnp.where(places >= end, end, first)

    _, first = lax.fori_loop(0, lens_ref.shape[0], later, (jnp.int32(0), jnp.zeros((1, rows), jnp.int32)))
    for side in range(2):
        keys = base - REACH * rows + side * half + lax.broadcasted_iota(jnp.int32, (span, half), 0)
        own = slice(side * half, (side + 1) * half)
        allowed = (keys >= first[:, own]) & (keys <= places[:, own])
        bias_ref[side] = jnp.where(allowed, 0.0, -1e30)
    ready()
    units = [(l, j) for l in range(2) for j in range(group)]
    chunks = [units[n:n + 2] for n in range(0, len(units), 2)]
    steps = [(side, n) for side in range(2) for n in range(len(chunks))]

    def operands(side, n):
        r = slice(side * half, (side + 1) * half)
        q = jnp.concatenate([held_ref[l, r, j * HD:(j + 1) * HD] for l, j in chunks[n]], axis=0)
        g = jnp.concatenate([held_ref[2 + l, r, j * HD:(j + 1) * HD] for l, j in chunks[n]], axis=0)
        return q, g

    def products(side, n):
        w = slice(side * half, side * half + span)
        q, g = operands(side, n)
        s = lax.dot_general(kv_ref[w, :HD], q, NT, preferred_element_type=jnp.float32)
        dp = lax.dot_general(kv_ref[w, HD:], g, NT, preferred_element_type=jnp.float32)
        return s, dp

    ahead = products(*steps[0])
    for at, (side, n) in enumerate(steps):
        s, dp = ahead
        if at + 1 < len(steps):
            ahead = products(*steps[at + 1])
        w = slice(side * half, side * half + span)
        r = slice(side * half, (side + 1) * half)
        bias = bias_ref[side]
        s = s * (scale * math.log2(math.e)) + jnp.concatenate([bias] * len(chunks[n]), axis=1)
        raised = jnp.exp2(s - jnp.max(s, axis=0, keepdims=True))
        p = raised * (1.0 / jnp.sum(raised, axis=0, keepdims=True))
        ph = p.astype(jnp.bfloat16)
        delta = jnp.sum(ph.astype(jnp.float32) * dp, axis=0, keepdims=True)
        ds = (p * (dp - delta)).astype(jnp.bfloat16)
        q, g = operands(side, n)
        if side == 0 and n == 0:
            acc_ref[span:, :] = jnp.zeros((half, 2 * HD), jnp.float32)
            acc_ref[w, HD:] = jnp.dot(ph, g, preferred_element_type=jnp.float32)
            acc_ref[w, :HD] = jnp.dot(ds, q, preferred_element_type=jnp.float32)
        else:
            acc_ref[w, HD:] += jnp.dot(ph, g, preferred_element_type=jnp.float32)
            acc_ref[w, :HD] += jnp.dot(ds, q, preferred_element_type=jnp.float32)
        dq = (jnp.dot(kt_ref[:, w], ds, preferred_element_type=jnp.float32) * scale).T.astype(jnp.bfloat16)
        for i, (l, j) in enumerate(chunks[n]):
            made_ref[l, r, j * HD:(j + 1) * HD] = dq[i * half:(i + 1) * half]


def attend_scratch(rows):
    keys = (REACH + 1) * rows
    return [pltpu.VMEM((keys, 2 * HD), jnp.bfloat16), pltpu.VMEM((HD, keys), jnp.bfloat16),
            pltpu.VMEM((2, keys - rows // 2, rows // 2), jnp.float32)]


def chosen(lane, kv_ref, i, ref, other):
    rows = ref.shape[0]
    if ref is other:
        kv_ref[i * rows:(i + 1) * rows, :] = ref[...]
        return

    @pl.when(lane == 0)
    def _():
        kv_ref[i * rows:(i + 1) * rows, :] = ref[...]

    @pl.when(lane == 1)
    def _():
        kv_ref[i * rows:(i + 1) * rows, :] = other[...]


def fetched(arrays, columns, held_ref, sems):
    copies = [pltpu.make_async_copy(ref.at[:, columns], held_ref.at[i], sems.at[i]) for i, ref in enumerate(arrays)]
    for copy in copies:
        copy.start()

    def ready():
        for copy in copies:
            copy.wait()

    return ready


def scaled(term):
    return jnp.concatenate([term[:, :HD] * (1.0 / math.sqrt(HD)), term[:, HD:]], axis=1)


def whole_kernel(head, rows, group, here_ref, lens_ref, q1, q2, g1, g2, b3, b2, b1, b0,
                 made_ref, f3_ref, f2_ref, f1_ref, own_ref, kv_ref, kt_ref, bias_ref, acc_ref, held_ref, sems):
    ready = fetched((q1, q2, g1, g2), slice(head * group * HD, (head + 1) * group * HD), held_ref, sems)
    for i, ref in enumerate((b3, b2, b1, b0)):
        kv_ref[i * rows:(i + 1) * rows, :] = ref[...]
    attend(rows, group, here_ref[0], lens_ref, kv_ref, kt_ref, bias_ref, acc_ref, held_ref, made_ref, ready)
    for i, ref in enumerate((f3_ref, f2_ref, f1_ref, own_ref)):
        ref[...] = scaled(acc_ref[i * rows:(i + 1) * rows, :]).astype(ref.dtype)


def split_kernel(here_ref, k, v, given_ref, mine_ref, sems):
    lane = here_ref[0] % 2
    copies = []
    for i, (head, ref) in enumerate(((1 - lane, given_ref), (lane, mine_ref))):
        columns = pl.ds(pl.multiple_of(head * HD, HD), HD)
        copies.append(pltpu.make_async_copy(k.at[:, columns], ref.at[:, :HD], sems.at[2 * i]))
        copies.append(pltpu.make_async_copy(v.at[:, columns], ref.at[:, HD:], sems.at[2 * i + 1]))
    for copy in copies:
        copy.start()
    for copy in copies:
        copy.wait()


def called(kernel, name, operands, kinds, outs, scratch, mebibytes=44):
    places = {"s": pltpu.SMEM, "v": pltpu.VMEM, "h": pltpu.HBM, "a": pl.ANY}
    return pl.pallas_call(
        kernel,
        in_specs=[pl.BlockSpec(memory_space=places[k]) for k in kinds],
        out_specs=[pl.BlockSpec(memory_space=pltpu.VMEM)] * len(outs),
        out_shape=[jax.ShapeDtypeStruct(shape, dtype) for shape, dtype in outs],
        scratch_shapes=scratch,
        compiler_params=pltpu.CompilerParams(vmem_limit_bytes=mebibytes * 1024 * 1024),
        cost_estimate=pl.CostEstimate(flops=1 << 15, bytes_accessed=1 << 15, transcendentals=0),
        name=name,
    )(*operands)


def moved(value, axis, place):
    pairs = [(i, place(i)) for i in range(lax.axis_size(axis))]
    return lax.ppermute(value, axis, [(i, j) for i, j in pairs if j is not None])


def after(value, *earlier):
    return lax.optimization_barrier((value,) + earlier)[0]


def gathered(kv_grads, heads, lanes):
    return [kv_grads] + [
        moved(kv_grads, "tok", lambda t, j=j: ((t // lanes) ^ j) * lanes + t % lanes) for j in range(1, heads)]


def line_rows(count, indices, paired, picks_ref, blocks, hids):
    line, head, mine = picks_ref[0], picks_ref[1], picks_ref[2]
    total = None
    for j, block in zip(indices, blocks):
        if paired:
            near = (line ^ j) % 2 == head % 2
            y = head // 2
            terms = []
            for e in range(2):
                slots = [4 * e + 2 * (y ^ q) + j // 2 for q in range(2)]
                pieces = [jnp.where(near, hids[0][slot], hids[1][slot]) for slot in slots]
                terms.append((jnp.concatenate(pieces, axis=1), block[mine ^ e]))
        else:
            slot, step = 0, 1
            while step < count:
                slot = 2 * slot + ((line ^ j ^ head) // step) % 2
                step *= 2
            terms = [(hids[0][slot], block[...])]
        for turned, grads in terms:
            term = jnp.dot(turned, grads, preferred_element_type=jnp.float32)
            total = term if total is None else total + term
    return total


def part_kernel(indices, picks_ref, *refs):
    n = len(indices)
    refs[-1][...] = line_rows(4, indices, True, picks_ref, refs[:n], refs[n:-1])


def project_kernel(count, indices, paired, picks_ref, *refs):
    own_ref, away_ref = refs[-2:]
    n = len(indices)
    total = line_rows(count, indices, paired, picks_ref, refs[:n], refs[n:-3] if paired else refs[n:-2])
    if paired:
        total = total + refs[-3][...]
    mine = picks_ref[2]
    lanes, part = away_ref.shape[0] + 1, own_ref.shape[0]
    own_ref[...] = jnp.zeros_like(own_ref)
    for d in range(lanes):
        piece = total[d * part:(d + 1) * part]

        @pl.when(mine == d)
        def _():
            own_ref[...] = piece

        for e in range(1, lanes):
            @pl.when((mine ^ e) == d)
            def _():
                away_ref[e - 1] = piece.astype(jnp.bfloat16)


def project(picks, hids, blocks, lanes, indices=None, before=None):
    rows, columns = hids[0].shape[-2], blocks[0].shape[-1]
    part = rows // lanes
    chosen_blocks = [blocks[j] for j in indices] if indices else blocks
    operands = [*chosen_blocks, *hids] + ([] if before is None else [before])
    if indices and before is None:
        return called(functools.partial(part_kernel, indices), "part", [picks, *operands], "s" + "v" * len(operands),
                      [((rows, columns), jnp.float32)], [])[0]
    return called(
        functools.partial(project_kernel, len(blocks), indices or range(len(blocks)), before is not None), "project",
        [picks, *operands], "s" + "v" * len(operands),
        [((part, columns), jnp.float32), ((lanes - 1, part, columns), jnp.bfloat16)], [])


def first_kernel(rows, group, here_ref, lens_ref, q1, q2, g1, g2, far, lifted, mine, got,
                 made_ref, acc_ref, kv_ref, kt_ref, bias_ref, held_ref, sems):
    lane = here_ref[0] % 2
    ready = fetched((q1, q2, g1, g2), pl.ds(pl.multiple_of(lane * group * HD, HD), group * HD), held_ref, sems)
    along, crosswise = lifted.at[0], lifted.at[1]
    for i, pair in enumerate(((far, crosswise), (along, along), (crosswise, got), (mine, mine))):
        chosen(lane, kv_ref, i, *pair)
    attend(rows, group, here_ref[0], lens_ref, kv_ref, kt_ref, bias_ref, acc_ref, held_ref, made_ref, ready)


def second_kernel(rows, group, here_ref, lens_ref, held_ref, far, lifted, mine, got, before_ref,
                  made_ref, far_ref, pair_ref, own_ref, kv_ref, kt_ref, bias_ref, acc_ref):
    lane = here_ref[0] % 2
    along, crosswise = lifted.at[0], lifted.at[1]
    for i, pair in enumerate(((along, far), (crosswise, crosswise), (mine, along), (got, got))):
        chosen(lane, kv_ref, i, *pair)
    attend(rows, group, here_ref[0] + 1 - 2 * lane, lens_ref, kv_ref, kt_ref, bias_ref, acc_ref, held_ref, made_ref, lambda: None)

    def merged(even_ref, odd_ref):
        block = lambda ref, i: ref[i * rows:(i + 1) * rows, :]
        far_ref[...] = scaled(block(even_ref, 0)).astype(far_ref.dtype)
        for i in range(2):
            pair_ref[i] = scaled(block(even_ref, 1 + i) + block(odd_ref, i)).astype(pair_ref.dtype)
        own_ref[0] = scaled(block(even_ref, 3) + block(odd_ref, 2))
        own_ref[1] = scaled(block(odd_ref, 3))

    @pl.when(lane == 0)
    def _():
        merged(before_ref, acc_ref)

    @pl.when(lane == 1)
    def _():
        merged(acc_ref, before_ref)


def general(place, line, lane, head, heads, tokens, lanes, kv_heads, lens, arrays, stacked, hidden_states):
    def crossed(i):
        t, h = i // heads, i % heads
        return (h * lanes + t % lanes) * heads + t // lanes

    hid = moved(hidden_states.T[None], ("tok", "head"), crossed)
    step = heads // 2
    while step:
        hid = jnp.concatenate([hid, moved(hid, "head", lambda h: h ^ step)], axis=0)
        step //= 2
    picks = jnp.stack([line, head, lane]).astype(jnp.int32)
    rows, width = arrays[0].shape
    group = width // (kv_heads * HD)
    block = (rows, 2 * HD)
    firsts, seconds, parts = [], [], []
    for c, own in enumerate(stacked):
        window = [moved(own, "tok", lambda t, s=s: t + s if t + s < tokens else None) for s in range(REACH, 0, -1)] + [own]
        made, *far, total = called(
            functools.partial(whole_kernel, c, rows, group), "attend", [place, lens, *arrays, *window],
            "ss" + "h" * 4 + "v" * 4,
            [((2, rows, group * HD), jnp.bfloat16)] + [(block, jnp.bfloat16)] * REACH + [(block, jnp.float32)],
            attend_scratch(rows) + [pltpu.VMEM(((REACH + 1) * rows, 2 * HD), jnp.float32),
                                    pltpu.VMEM((4, rows, group * HD), jnp.bfloat16), pltpu.SemaphoreType.DMA((4,))])
        firsts.append(made[0])
        seconds.append(made[1])
        for s in range(1, REACH + 1):
            back = moved(far[REACH - s], "tok", lambda t, s=s: t - s if t >= s else None)
            total = total + back.astype(jnp.float32)
        mine, away = project(picks, [hid], gathered(total.astype(jnp.bfloat16), heads, lanes), lanes)
        for d in range(1, lanes):
            mine = mine + moved(away[d - 1], "tok", lambda t, d=d: t ^ d).astype(jnp.float32)
        parts.append(mine)
    return tuple(jnp.concatenate(x, axis=1) for x in (firsts, seconds, parts))


def paired(place, line, lane, head, heads, tokens, lanes, kv_heads, lens, arrays, stacked, hidden_states):
    both = ("tok", "head")
    rows, width = arrays[0].shape
    group = width // (kv_heads * HD)
    wide = group * HD
    even = lane == 0

    def mine_and_other(a, b):
        return jnp.where(even, a, b), jnp.where(even, b, a)

    def up(value, lines):
        return moved(value, "tok", lambda t: t + lines * lanes if t + lines * lanes < tokens else None)

    def down(value, lines):
        return moved(value, "tok", lambda t: t - lines * lanes if t >= lines * lanes else None)

    def over(value):
        return moved(value, "tok", lambda t: t ^ 1)

    def crossed(flip):
        def place_of(i):
            t, h = i // heads, i % heads
            z, c = t // lanes, h % 2
            return (((z // 2) ^ flip) * 2 + c) * lanes * heads + (t % lanes) * heads + (h // 2) * 2 + z % 2
        return place_of

    y = head // 2
    half = rows // 2
    given, mine = called(split_kernel, "split", [place, *stacked], "shh", [((rows, 2 * HD), jnp.bfloat16)] * 2,
                         [pltpu.SemaphoreType.DMA((4,))], 60)
    got = over(given)
    asked = over(jnp.stack([jnp.where(even, a[:, wide:], a[:, :wide]) for a in (after(x, given) for x in arrays)]))
    risen = jnp.stack([mine, got])
    lifted = up(risen, 1)
    far = up(jnp.where(even, got, mine), 2)
    kept, lent = (lax.dynamic_slice_in_dim(after(hidden_states, given), at * half, half, 0) for at in (y, 1 - y))
    lent = moved(lent, "head", lambda h: h ^ 2)
    own_line = (line // 2) == y
    afar = moved(after(jnp.where(own_line, lent, kept), lifted, far), both, crossed(1))
    window = [far, lifted, mine, got]
    keys = (REACH + 1) * rows
    made, sums = called(
        functools.partial(first_kernel, rows, group), "attend_own", [place, lens, *arrays, *window], "ss" + "h" * 4 + "v" * 4,
        [((2, rows, wide), jnp.bfloat16), ((keys, 2 * HD), jnp.float32)],
        attend_scratch(rows) + [pltpu.VMEM((4, rows, wide), jnp.bfloat16), pltpu.SemaphoreType.DMA((4,))])
    nearby = moved(after(jnp.where(own_line, kept, lent), sums), both, crossed(0))
    made_other, farther, nearer, own = called(
        functools.partial(second_kernel, rows, group), "attend_other", [place, lens, asked, *window, after(sums, afar)],
        "ss" + "v" * 6,
        [((2, rows, wide), jnp.bfloat16), ((rows, 2 * HD), jnp.bfloat16), ((2, rows, 2 * HD), jnp.bfloat16),
         ((2, rows, 2 * HD), jnp.float32)],
        attend_scratch(rows) + [pltpu.VMEM((keys, 2 * HD), jnp.float32)])
    one, two = down(nearer, 1), down(farther, 2)
    sent = over(made_other)
    hops = jnp.swapaxes(jnp.stack([nearby, after(afar, own)]), 1, 2)
    beside, upright = over(hops), moved(hops, "head", lambda h: h ^ 2)
    skew = moved(after(beside, one), "head", lambda h: h ^ 2)
    total = (own + one.astype(jnp.float32)).at[1].add(two.astype(jnp.float32)).astype(jnp.bfloat16)
    across = moved(total, "tok", lambda t: t ^ (2 * lanes))
    j1 = moved(total, "tok", lambda t: t ^ lanes)
    blocks = [total, j1, across, moved(after(across, j1), "tok", lambda t: t ^ lanes)]
    hids = jnp.concatenate([after(hops, j1, across, sent), upright, beside, skew], axis=0)
    picks = jnp.stack([line, head, lane]).astype(jnp.int32)
    hids = [hids, moved(hids, "head", lambda h: h ^ 1)]
    part = project(picks, hids, blocks, lanes, (0, 1, 2))
    kept, away = project(picks, hids, blocks, lanes, (3,), part)
    came = over(away[0]).astype(jnp.float32)
    firsts, seconds = (jnp.concatenate(mine_and_other(made[l], sent[l]), axis=1) for l in range(2))
    return (firsts, seconds, jnp.concatenate(mine_and_other(kept, came), axis=1))


def body(queries_first, queries_second, grads_first, grads_second, key_states, value_states, doc_lengths, hidden_states):
    kv_heads = key_states.shape[1] // HD
    tokens, heads = lax.axis_size("tok"), lax.axis_size("head")
    lanes = tokens // heads
    here, head = lax.axis_index("tok"), lax.axis_index("head")
    arrays = (queries_first, queries_second, grads_first, grads_second)
    if (lanes, heads, kv_heads, REACH) == (2, 4, 2, 3):
        plan, stacked = paired, [key_states, value_states]
    else:
        plan = general
        stacked = [jnp.concatenate([x[:, c * HD:(c + 1) * HD] for x in (key_states, value_states)], axis=1)
                   for c in range(kv_heads)]
    return plan(here.reshape(1).astype(jnp.int32), here // lanes, here % lanes, head, heads, tokens, lanes, kv_heads,
                doc_lengths, arrays, stacked, hidden_states)


def solution(mesh):
    split = P("tok", "head")
    return jax.shard_map(
        body,
        mesh=mesh,
        in_specs=(split,) * 6 + (P(), split),
        out_specs=(split,) * 3,
        check_vma=False,
    )
```
